32 devices in a mesh: grp: 2 (over y), lat: 4 (over z), lev: 2 (over x), fld: 2 (over core).
Axes of the slice: x: 2, y: 2, z: 4, core: 2. Of those that a mesh axis runs over, the one named last changes fastest.
Arguments:
- upstream: bfloat16 [16, 4, 1024, 2048], P('grp', 'fld', 'lat', 'lev'), parts along dimension 0, may hold values from -6 to 6
- departure: int32 [16, 1024, 2048], P('grp', 'lat', 'lev'), parts along dimension 0, may hold values from 0 to 3
- fractions: bfloat16 [2, 16, 1024, 2048], P(None, 'grp', 'lat', 'lev'), parts along dimension 1, may hold values from 0 to 1
- heating: bfloat16 [8, 1024, 2048], P(('grp', 'fld'), 'lat', 'lev'), parts along dimension 0, may hold values from -6 to 6
- mixing: float32 [4, 8, 8], P('fld'), may hold values from -2 to 2
- slot_wavenumber: int32 [8], replicated, may hold values from 0 to 7, as said below
- legendre: bfloat16 [8, 1024, 1024], P('lat', None, 'lev'), as said below
Outputs:
- spectrum: float32 [8, 1024, 4, 4, 8], P('lat', 'lev', 'grp', 'fld'), parts along dimension 2
The draws below stay inside these ranges and needn't reach their ends.
There are 2 independent parts, one for each index of `grp`. The reference program is written for one: setup_inputs(seed, part) draws one part's arguments, and reference() takes and returns one part's arrays. A program takes and returns all parts, laid end to end along the dimension named above; an argument that names none is the same for every part. Nothing has to cross between parts.
Inputs may be any that keep to these rules, and one draw needn't show every extreme that they name: `slot_wavenumber`: each value appears exactly once. legendre[s, i, n] is the fully normalized associated Legendre function of degree n and order m_s at cos(theta_i), theta_i = (i + 0.5) pi / 1024, times sqrt(pi sin(theta_i) / 1024), zero for n < m_s, rounded to bfloat16.
All inputs are finite; a program needn't handle non-finite values.
Results may differ from the reference program's by a relative error of at most 0.0043.
Values may be sent and summed in bfloat16 or wider, within the bound.
A program may use at most 768 MiB of HBM per device.

```python
import math
import jax
import jax.numpy as jnp
from jax import lax

NLAT = 1024
NLON = 2048
NTRUNC = 1024
VARS = 4
LEVS = 8
M_WIN = 8


def wave_order(key):
    return jax.random.permutation(jax.random.fold_in(key, 7), M_WIN).astype(jnp.int32)


def draw_slot_wavenumber(key, part):
    return wave_order(key)


def draw_legendre(key, part):
    order = wave_order(key)
    orders = (order * (NTRUNC // M_WIN)).astype(jnp.float32)[:, None]
    theta = (jnp.arange(NLAT, dtype=jnp.float32) + 0.5) * (math.pi / NLAT)
    cosine = jnp.cos(theta)[None, :]
    sine = jnp.sin(theta)[None, :]
    log_start = 0.5 * math.log(0.5) + 0.5 * (jax.scipy.special.gammaln(orders + 1.5) - jax.scipy.special.gammaln(jnp.float32(1.5)) - jax.scipy.special.gammaln(orders + 1.0)) + orders * jnp.log(sine)
    start_value = jnp.exp(log_start)
    quadrature = jnp.sqrt(math.pi * sine / NLAT)

    def advance(carry, degree):
        latest, before = carry
        level = degree.astype(jnp.float32)
        denominator = jnp.maximum((level - orders) * (level + orders), 1.0)
        factor_a = jnp.sqrt((2.0 * level + 1.0) * (2.0 * level - 1.0) / denominator)
        factor_b = jnp.sqrt(jnp.maximum((2.0 * level + 1.0) * (level + orders - 1.0) * (level - orders - 1.0), 0.0) / (jnp.maximum(2.0 * level - 3.0, 1.0) * denominator))
        recursed = factor_a * cosine * latest - factor_b * before
        value = jnp.where(level < orders, 0.0, jnp.where(level == orders, start_value, recursed))
        return ((value, latest), value * quadrature)
    zeros = jnp.zeros((M_WIN, NLAT), jnp.float32)
    _, table = lax.scan(advance, (zeros, zeros), jnp.arange(NTRUNC, dtype=jnp.int32))
    return jnp.transpose(table, (1, 2, 0)).astype(jnp.bfloat16)


def touch_ends(drawn, rng, smallest, top_value):
    longest = drawn.shape.index(max(drawn.shape))
    spots = []
    for shift in (0, 1):
        where = [jax.random.randint(jax.random.fold_in(rng, axis), (), 0, length) for axis, length in enumerate(drawn.shape)]
        where[longest] = (where[longest] + shift) % drawn.shape[longest]
        spots.append(tuple(where))
    return drawn.at[spots[0]].set(smallest).at[spots[1]].set(top_value)


def levels(stream_key, shape, cuts, smallest, largest):
    loudness = 1.0
    for axis_at, shards_of in cuts:
        steps = jax.random.uniform(jax.random.fold_in(jax.random.fold_in(stream_key, 6), axis_at), (shards_of,), jnp.float32, smallest / len(cuts), largest / len(cuts))
        loudness = loudness * jnp.repeat(jnp.exp(steps), shape[axis_at] // shards_of).reshape((-1,) + (1,) * (len(shape) - 1 - axis_at))
    return loudness


def normal_values(own_key, dims, deviation, reach, split=(), held_as=jnp.bfloat16):
    drawn = deviation * jax.random.normal(own_key, dims, jnp.float32)
    if split:
        drawn = drawn * levels(own_key, dims, split, -0.22, 0.18)
    return jnp.clip(drawn, -reach, reach).astype(held_as)


def setup_inputs(seed: int = 0, part: int = 0) -> dict:
    key_list = jax.random.split(jax.random.key(seed), 8)
    part_splits = jax.random.split(jax.random.fold_in(key_list[7], part), 8)
    return {
        "upstream": normal_values(part_splits[0], (LEVS, VARS, NLAT, NLON), 1.0, 6.0, ((1, 2), (2, 4), (3, 2))),
        "departure": touch_ends(jax.random.randint(part_splits[1], (LEVS, NLAT, NLON), 0, 4), jax.random.fold_in(part_splits[1], 1), 0, 3).astype(jnp.int32),
        "fractions": jnp.clip(1.0 * jax.random.uniform(part_splits[2], (2, LEVS, NLAT, NLON), jnp.float32) ** levels(part_splits[2], (2, LEVS, NLAT, NLON), ((2, 4), (3, 2)), -0.2, 0.2), 0.0, 1.0).astype(jnp.bfloat16),
        "heating": normal_values(part_splits[3], (VARS, NLAT, NLON), 1.0, 6.0, ((0, 2), (1, 4), (2, 2))),
        "mixing": normal_values(key_list[4], (VARS, LEVS, LEVS), LEVS ** -0.5, 2.0, ((0, 2),), jnp.float32),
        "slot_wavenumber": draw_slot_wavenumber(jax.random.fold_in(key_list[7], 71), part),
        "legendre": draw_legendre(jax.random.fold_in(key_list[7], 71), part),
    }


def cubic_weights(fraction):
    return [-fraction * (fraction - 1.0) * (fraction - 2.0) / 6.0, (fraction + 1.0) * (fraction - 1.0) * (fraction - 2.0) / 2.0, -(fraction + 1.0) * fraction * (fraction - 2.0) / 2.0, (fraction + 1.0) * fraction * (fraction - 1.0) / 6.0]

def fourier_basis(first, count, waves):
    positions = first + jnp.arange(count, dtype=jnp.int32)
    phase = positions[:, None] * waves[None, :] % NLON
    angle = phase.astype(jnp.float32) * (2.0 * math.pi / NLON)
    return jnp.concatenate([jnp.cos(angle), -jnp.sin(angle)], axis=1).astype(jnp.bfloat16)

def level_interp(inputs):
    field, code, frac_lat, frac_lon = inputs
    wrapped = jnp.concatenate([field[:, :, -3:], field, field[:, :, :3]], axis=2)
    padded = jnp.pad(wrapped, ((0, 0), (3, 3), (0, 0)))
    width = NLON + 6
    flat = padded.reshape(VARS, -1)
    shift_lat = code // 2 - 1
    shift_lon = code % 2 - 1
    row_index = jnp.arange(NLAT, dtype=jnp.int32)[:, None]
    col_index = jnp.arange(NLON, dtype=jnp.int32)[None, :]
    anchor = (row_index + 3 + shift_lat) * width + col_index + 3 + shift_lon
    weights_lat = cubic_weights(frac_lat.astype(jnp.float32))
    weights_lon = cubic_weights(frac_lon.astype(jnp.float32))
    total = jnp.zeros((VARS, NLAT, NLON), jnp.float32)
    for row_tap in range(4):
        for col_tap in range(4):
            offset = (row_tap - 1) * width + col_tap - 1
            picked = flat[:, (anchor + offset).reshape(-1)].reshape(VARS, NLAT, NLON)
            total = total + (weights_lat[row_tap] * weights_lon[col_tap])[None] * picked.astype(jnp.float32)
    return total

def reference(upstream, departure, fractions, heating, mixing, slot_wavenumber, legendre):
    interp = lax.map(level_interp, (upstream, departure, fractions[0], fractions[1]))
    column = jnp.einsum('vlk,kvij->lvij', mixing, interp, precision=lax.Precision.HIGHEST)
    state = (interp + heating[None].astype(jnp.float32) * jnp.tanh(column)).astype(jnp.bfloat16)
    waves = slot_wavenumber * (NTRUNC // M_WIN)
    sums = jnp.dot(state.reshape(-1, NLON), fourier_basis(0, NLON, waves), preferred_element_type=jnp.float32)
    coefficients = (sums * (1.0 / math.sqrt(NLON))).astype(jnp.bfloat16).reshape(LEVS, VARS, NLAT, 2, M_WIN)
    return jnp.einsum('sin,lvirs->snrvl', legendre.astype(jnp.float32), coefficients.astype(jnp.float32), precision=lax.Precision.HIGHEST)
```

```python
import math

import jax
import jax.numpy as jnp
from jax import lax
from jax.experimental import pallas as pl
from jax.experimental.pallas import tpu as pltpu
from jax.sharding import PartitionSpec as P

NLON = 2048
NTRUNC = 1024
ROWS = 32
BLOCKS = 8
LANES = 128


def with_halo(shard, sides, width, wrap):
    for axis, dim in sides:
        peers, length = (lax.axis_size(axis), shard.shape[dim])
        up = [(i, (i + 1) % peers) for i in range(peers if wrap else peers - 1)]
        down = [(j, i) for i, j in up]
        last = lax.slice_in_dim(shard, length - width, length, axis=dim)
        leading = lax.slice_in_dim(shard, 0, width, axis=dim)
        before = lax.ppermute(last, axis, up)
        after = lax.ppermute(leading, axis, down)
        shard = jnp.concatenate([before, shard, after], axis=dim)
    return shard


def cubic_weights(fraction):
    return [
        -fraction * (fraction - 1.0) * (fraction - 2.0) / 6.0,
        (fraction + 1.0) * (fraction - 1.0) * (fraction - 2.0) / 2.0,
        -(fraction + 1.0) * fraction * (fraction - 2.0) / 2.0,
        (fraction + 1.0) * fraction * (fraction - 1.0) / 6.0,
    ]


def offset_weights(shift, weights):
    result = []
    for target in range(-2, 3):
        total = jnp.zeros(shift.shape, jnp.float32)
        for tap in range(4):
            total = total + jnp.where(shift + tap - 1 == target, weights[tap], 0.0)
        result.append(total)
    return jnp.stack(result)


def fourier_basis(first, count, waves):
    positions = first + jnp.arange(count, dtype=jnp.int32)
    phase = positions[:, None] * waves[None, :] % NLON
    angle = phase.astype(jnp.float32) * (2.0 * math.pi / NLON)
    return jnp.concatenate([jnp.cos(angle), -jnp.sin(angle)], axis=1).astype(jnp.bfloat16)


def shards_plain(upstream, departure, fractions, heating, mixing, slot_wavenumber, legendre):
    levels, var_dev, lat_dev, lon_dev = upstream.shape
    widened = with_halo(upstream, (("lev", 3),), 2, True)
    padded = with_halo(widened, (("lat", 2),), 2, False)
    shift_lat = departure // 2 - 1
    shift_lon = departure % 2 - 1
    row_weights = offset_weights(shift_lat, cubic_weights(fractions[0].astype(jnp.float32)))
    col_weights = offset_weights(shift_lon, cubic_weights(fractions[1].astype(jnp.float32)))
    row_sums = []
    for row_off in range(5):
        windows = jnp.stack(
            [
                padded[:, :, row_off : row_off + lat_dev, col_off : col_off + lon_dev]
                for col_off in range(5)
            ]
        )
        row_sums.append(jnp.sum(windows.astype(jnp.float32) * col_weights[:, :, None], axis=0))
    interp = jnp.sum(jnp.stack(row_sums) * row_weights[:, :, None], axis=0)
    column = jnp.einsum("vlk,kvij->lvij", mixing, interp, precision=lax.Precision.HIGHEST)
    state = (interp + heating[None].astype(jnp.float32) * jnp.tanh(column)).astype(jnp.bfloat16)
    m_window = slot_wavenumber.shape[0]
    waves = slot_wavenumber * (NTRUNC // m_window)
    local_basis = fourier_basis(lax.axis_index("lev") * lon_dev, lon_dev, waves)
    sums = lax.psum_scatter(
        jnp.dot(
            state.reshape(-1, lon_dev), local_basis, preferred_element_type=jnp.float32
        ).reshape(
            levels // lax.axis_size("lev") * lax.axis_size("lev"), var_dev, lat_dev, 2 * m_window
        ),
        "lev",
        scatter_dimension=0,
        tiled=True,
    )
    coefficients = (
        (sums * (1.0 / math.sqrt(NLON)))
        .astype(jnp.bfloat16)
        .reshape(-1, var_dev, lat_dev, 2, m_window)
    )
    owned = lax.all_to_all(coefficients, "lat", split_axis=4, concat_axis=2, tiled=True)
    return jnp.einsum(
        "sin,lvirs->snrvl",
        legendre,
        lax.all_gather(owned, "lev", axis=0, tiled=True),
        preferred_element_type=jnp.float32,
    )


def axis_weights(x):
    square = x * x
    cubic = x * (square - 1.0) * (1.0 / 6.0)
    right = jnp.where(x > 0.0, cubic, 0.0)
    half = 0.5 * square
    half_x = 0.5 * x
    inner = half - 4.0 * right
    triple = 3.0 * cubic
    return [
        right - cubic,
        inner + (triple - half_x),
        (1.0 - square) + (6.0 * right - triple),
        inner + (half_x + cubic),
        right,
    ]


def column_kernel(
    main, prev, following, e_main, e_prev, e_following, top, bottom, departure, fractions,
    heating, coupling, basis, out, turned, edges, images, nearest, position, interp, state,
):
    levels, variables = main.shape[0], main.shape[1]
    rows = main.shape[2]
    pack = variables * BLOCKS
    block = pl.program_id(0)
    first = block == 0
    last = block == pl.num_programs(0) - 1
    lane = lax.broadcasted_iota(jnp.int32, (variables, BLOCKS, LANES), 2)
    sub = lax.broadcasted_iota(jnp.int32, (variables, BLOCKS, LANES), 1)

    def turn(values, start, v):
        count = values.shape[0]
        for jb in range(BLOCKS):
            turned[pl.ds(start * pack + v * BLOCKS + jb, count, stride=pack), :] = values[
                :, jb * LANES : (jb + 1) * LANES
            ]

    def one_level(l, carry):
        for v in range(variables):
            width = BLOCKS * LANES
            turn(main[l, v].astype(jnp.float32), 8, v)
            before = prev[l, v].astype(jnp.float32)[8:16]
            turn(jnp.where(first, top[l, v, :, :width], before), 0, v)
            after = following[l, v].astype(jnp.float32)[0:8]
            turn(jnp.where(last, bottom[l, v, :, :width], after), 8 + rows, v)
            edges[v, 8 : 8 + rows] = e_main[l, v].astype(jnp.float32)
            before = e_prev[l, v].astype(jnp.float32)[8:16]
            edges[v, 0:8] = jnp.where(first, top[l, v, :, width:], before)
            after = e_following[l, v].astype(jnp.float32)[0:8]
            edges[v, 8 + rows : 16 + rows] = jnp.where(last, bottom[l, v, :, width:], after)
        code = departure[l]
        t_lat = fractions[0, l].astype(jnp.float32)
        t_lon = fractions[1, l].astype(jnp.float32)
        y = jnp.where(code >= 2, t_lat, t_lat - 1.0)
        x = jnp.where((code & 1) == 1, t_lon, t_lon - 1.0)
        for jb in range(BLOCKS):
            lanes = slice(jb * LANES, (jb + 1) * LANES)
            position[0, pl.ds(jb, rows, stride=BLOCKS), :] = y[:, lanes]
            position[1, pl.ds(jb, rows, stride=BLOCKS), :] = x[:, lanes]

        def make_images(w, carry):
            at = pl.multiple_of((w + 6) * pack, pack)
            values = turned[pl.ds(at, pack), :].reshape(variables, BLOCKS, LANES)
            edge = jnp.stack(
                [
                    jnp.broadcast_to(edges[v, pl.ds(w + 6, 1), :], (BLOCKS, LANES))
                    for v in range(variables)
                ]
            )
            ahead = jnp.where(sub == BLOCKS - 1, edge, pltpu.roll(values, BLOCKS - 1, 1))
            behind = jnp.where(sub == 0, edge, pltpu.roll(values, 1, 1))
            shifted = [
                pltpu.roll(jnp.where(lane >= LANES - 2, behind, values), 2, 2),
                pltpu.roll(jnp.where(lane >= LANES - 1, behind, values), 1, 2),
                values,
                pltpu.roll(jnp.where(lane < 1, ahead, values), LANES - 1, 2),
                pltpu.roll(jnp.where(lane < 2, ahead, values), LANES - 2, 2),
            ]
            for q in range(5):
                image = shifted[q].reshape(pack, LANES)
                images[q, w] = image.astype(jnp.bfloat16)
                if q in (1, 2, 3):
                    nearest[q - 1, w] = image
            return carry

        lax.fori_loop(0, rows + 4, make_images, 0, unroll=4)

        def interpolate(i, carry):
            at = pl.multiple_of(i * BLOCKS, BLOCKS)
            row_w = axis_weights(position[0, pl.ds(at, BLOCKS), :])
            col_w = axis_weights(position[1, pl.ds(at, BLOCKS), :])
            row_w = [jnp.concatenate([w] * variables, axis=0) for w in row_w]
            col_w = [jnp.concatenate([w] * variables, axis=0) for w in col_w]
            row_n = [w.astype(jnp.bfloat16) for w in row_w]
            col_n = [w.astype(jnp.bfloat16) for w in col_w]
            outer = inner = None
            for r in range(5):
                line = col_n[0] * images[0, i + r] + col_n[4] * images[4, i + r]
                if r in (0, 4):
                    middle = [col_n[q] * images[q, i + r] for q in (1, 2, 3)]
                    line = (middle[0] + middle[1]) + (middle[2] + line)
                else:
                    near = [col_w[q] * nearest[q - 1, i + r] for q in (1, 2, 3)]
                    near = row_w[r] * (near[0] + near[1] + near[2])
                    inner = near if inner is None else inner + near
                line = row_n[r] * line
                outer = line if outer is None else outer + line
            total = inner + outer.astype(jnp.float32)
            interp[l, pl.ds(pl.multiple_of(i * pack, pack), pack), :] = total
            return carry

        lax.fori_loop(0, rows, interpolate, 0, unroll=4)
        return carry

    lax.fori_loop(0, levels, one_level, 0)

    for v in range(variables):
        for jb in range(BLOCKS):
            lanes = slice(jb * LANES, (jb + 1) * LANES)
            field = jnp.concatenate(
                [interp[l, pl.ds(v * BLOCKS + jb, rows, stride=pack), :] for l in range(levels)],
                axis=0,
            )
            column = jnp.dot(
                coupling[v], field.astype(jnp.bfloat16), preferred_element_type=jnp.float32
            )
            heat = jnp.concatenate([heating[v, :, lanes].astype(jnp.float32)] * levels, axis=0)
            state[:, lanes] = (field + heat * jnp.tanh(column)).astype(jnp.bfloat16)
        out[v, 0] = lax.dot_general(
            basis[...], state[...], (((1,), (1,)), ((), ())), preferred_element_type=jnp.float32
        )


def step_sums(upstream, departure, fractions, heating, mixing, basis):
    levels, variables, lat_dev, lon_dev = upstream.shape
    rows, near = ROWS, 16
    steps = lat_dev // rows
    peers = lax.axis_size("lev")
    up = [(i, (i + 1) % peers) for i in range(peers)]
    down = [(j, i) for i, j in up]
    left = lax.ppermute(upstream[..., lon_dev - 2 :], "lev", up)
    right = lax.ppermute(upstream[..., :2], "lev", down)
    gap = jnp.zeros((levels, variables, lat_dev, LANES - 4), upstream.dtype)
    edge = jnp.concatenate([right, gap, left], axis=3)
    bands = lax.axis_size("lat")
    north = [(i, i + 1) for i in range(bands - 1)]
    south = [(j, i) for i, j in north]
    lower = jnp.concatenate([upstream[:, :, lat_dev - 2 :], edge[:, :, lat_dev - 2 :]], axis=3)
    upper = jnp.concatenate([upstream[:, :, :2], edge[:, :, :2]], axis=3)
    top = lax.ppermute(lower, "lat", north).astype(jnp.float32)
    bottom = lax.ppermute(upper, "lat", south).astype(jnp.float32)
    top = jnp.pad(top, ((0, 0), (0, 0), (6, 0), (0, 0)))
    bottom = jnp.pad(bottom, ((0, 0), (0, 0), (0, 6), (0, 0)))
    unit = jnp.eye(rows, dtype=jnp.float32)
    coupling = (mixing[:, :, None, :, None] * unit[None, None, :, None, :]).reshape(
        variables, levels * rows, levels * rows
    )
    ratio = rows // near
    ends = lat_dev // near - 1

    def around(width):
        return [
            pl.BlockSpec((levels, variables, rows, width), lambda b: (0, 0, b, 0)),
            pl.BlockSpec(
                (levels, variables, near, width),
                lambda b: (0, 0, jnp.maximum(b * ratio - 1, 0), 0),
            ),
            pl.BlockSpec(
                (levels, variables, near, width),
                lambda b: (0, 0, jnp.minimum((b + 1) * ratio, ends), 0),
            ),
        ]

    def whole(shape):
        return pl.BlockSpec(shape, lambda b: (0,) * len(shape))

    pack = variables * BLOCKS
    slots = basis.shape[0]
    return pl.pallas_call(
        column_kernel,
        grid=(steps,),
        out_shape=jax.ShapeDtypeStruct((variables, steps, slots, levels * rows), jnp.float32),
        in_specs=around(lon_dev)
        + around(LANES)
        + [
            whole(top.shape),
            whole(bottom.shape),
            pl.BlockSpec((levels, rows, lon_dev), lambda b: (0, b, 0)),
            pl.BlockSpec((2, levels, rows, lon_dev), lambda b: (0, 0, b, 0)),
            pl.BlockSpec((variables, rows, lon_dev), lambda b: (0, b, 0)),
            whole(coupling.shape),
            whole(basis.shape),
        ],
        out_specs=pl.BlockSpec((variables, 1, slots, levels * rows), lambda b: (0, b, 0, 0)),
        scratch_shapes=[
            pltpu.VMEM(((rows + 16) * pack, LANES), jnp.float32),
            pltpu.VMEM((variables, rows + 16, LANES), jnp.float32),
            pltpu.VMEM((5, rows + 4, pack, LANES), jnp.bfloat16),
            pltpu.VMEM((3, rows + 4, pack, LANES), jnp.float32),
            pltpu.VMEM((2, rows * BLOCKS, LANES), jnp.float32),
            pltpu.VMEM((levels, rows * pack, LANES), jnp.float32),
            pltpu.VMEM((levels * rows, lon_dev), jnp.bfloat16),
        ],
        compiler_params=pltpu.CompilerParams(vmem_limit_bytes=48 * 1024 * 1024),
    )(
        upstream, upstream, upstream, edge, edge, edge, top, bottom, departure, fractions,
        heating, coupling.astype(jnp.bfloat16), basis,
    )


def shards(upstream, departure, fractions, heating, mixing, slot_wavenumber, legendre):
    levels, var_dev, lat_dev, lon_dev = upstream.shape
    if lon_dev != BLOCKS * LANES or lat_dev % ROWS or var_dev * BLOCKS != 16:
        return shards_plain(
            upstream, departure, fractions, heating, mixing, slot_wavenumber, legendre
        )
    m_window = slot_wavenumber.shape[0]
    waves = slot_wavenumber * (NTRUNC // m_window)
    basis = fourier_basis(lax.axis_index("lev") * lon_dev, lon_dev, waves).T
    partial = step_sums(upstream, departure, fractions, heating, mixing, basis)
    partial = partial.reshape(var_dev, lat_dev // ROWS, 2 * m_window, levels, ROWS)
    partial = partial.transpose(3, 0, 1, 4, 2).reshape(levels, var_dev, lat_dev, 2 * m_window)
    sums = lax.psum_scatter(partial, "lev", scatter_dimension=0, tiled=True)
    coefficients = (
        (sums * (1.0 / math.sqrt(NLON)))
        .astype(jnp.bfloat16)
        .reshape(-1, var_dev, lat_dev, 2, m_window)
    )
    owned = lax.all_to_all(coefficients, "lat", split_axis=4, concat_axis=2, tiled=True)
    return jnp.einsum(
        "sin,lvirs->snrvl",
        legendre,
        lax.all_gather(owned, "lev", axis=0, tiled=True),
        preferred_element_type=jnp.float32,
    )


def solution(mesh):
    in_specs = (
        P("grp", "fld", "lat", "lev"),
        P("grp", "lat", "lev"),
        P(None, "grp", "lat", "lev"),
        P(("grp", "fld"), "lat", "lev"),
        P("fld", None, None),
        P(),
        P("lat", None, "lev"),
    )
    out_specs = P("lat", "lev", "grp", "fld", None)
    return jax.shard_map(shards, mesh=mesh, in_specs=in_specs, out_specs=out_specs, check_vma=False)
```

```python
import math

import jax
import jax.numpy as jnp
from jax import lax
from jax.experimental import pallas as pl
from jax.experimental.pallas import tpu as pltpu
from jax.sharding import PartitionSpec as P

NLON = 2048
NTRUNC = 1024
ROWS = 32
BLOCKS = 8
LANES = 128
PITCH = 9


def with_halo(shard, sides, width, wrap):
    for axis, dim in sides:
        peers, length = (lax.axis_size(axis), shard.shape[dim])
        up = [(i, (i + 1) % peers) for i in range(peers if wrap else peers - 1)]
        down = [(j, i) for i, j in up]
        last = lax.slice_in_dim(shard, length - width, length, axis=dim)
        leading = lax.slice_in_dim(shard, 0, width, axis=dim)
        before = lax.ppermute(last, axis, up)
        after = lax.ppermute(leading, axis, down)
        shard = jnp.concatenate([before, shard, after], axis=dim)
    return shard


def cubic_weights(fraction):
    return [
        -fraction * (fraction - 1.0) * (fraction - 2.0) / 6.0,
        (fraction + 1.0) * (fraction - 1.0) * (fraction - 2.0) / 2.0,
        -(fraction + 1.0) * fraction * (fraction - 2.0) / 2.0,
        (fraction + 1.0) * fraction * (fraction - 1.0) / 6.0,
    ]


def offset_weights(shift, weights):
    result = []
    for target in range(-2, 3):
        total = jnp.zeros(shift.shape, jnp.float32)
        for tap in range(4):
            total = total + jnp.where(shift + tap - 1 == target, weights[tap], 0.0)
        result.append(total)
    return jnp.stack(result)


def fourier_basis(first, count, waves):
    positions = first + jnp.arange(count, dtype=jnp.int32)
    phase = positions[:, None] * waves[None, :] % NLON
    angle = phase.astype(jnp.float32) * (2.0 * math.pi / NLON)
    return jnp.concatenate([jnp.cos(angle), -jnp.sin(angle)], axis=1).astype(jnp.bfloat16)


def shards_plain(upstream, departure, fractions, heating, mixing, slot_wavenumber, legendre):
    levels, var_dev, lat_dev, lon_dev = upstream.shape
    widened = with_halo(upstream, (("lev", 3),), 2, True)
    padded = with_halo(widened, (("lat", 2),), 2, False)
    shift_lat = departure // 2 - 1
    shift_lon = departure % 2 - 1
    row_weights = offset_weights(shift_lat, cubic_weights(fractions[0].astype(jnp.float32)))
    col_weights = offset_weights(shift_lon, cubic_weights(fractions[1].astype(jnp.float32)))
    row_sums = []
    for row_off in range(5):
        windows = jnp.stack(
            [
                padded[:, :, row_off : row_off + lat_dev, col_off : col_off + lon_dev]
                for col_off in range(5)
            ]
        )
        row_sums.append(jnp.sum(windows.astype(jnp.float32) * col_weights[:, :, None], axis=0))
    interp = jnp.sum(jnp.stack(row_sums) * row_weights[:, :, None], axis=0)
    column = jnp.einsum("vlk,kvij->lvij", mixing, interp, precision=lax.Precision.HIGHEST)
    state = (interp + heating[None].astype(jnp.float32) * jnp.tanh(column)).astype(jnp.bfloat16)
    m_window = slot_wavenumber.shape[0]
    waves = slot_wavenumber * (NTRUNC // m_window)
    local_basis = fourier_basis(lax.axis_index("lev") * lon_dev, lon_dev, waves)
    sums = lax.psum_scatter(
        jnp.dot(
            state.reshape(-1, lon_dev), local_basis, preferred_element_type=jnp.float32
        ).reshape(
            levels // lax.axis_size("lev") * lax.axis_size("lev"), var_dev, lat_dev, 2 * m_window
        ),
        "lev",
        scatter_dimension=0,
        tiled=True,
    )
    coefficients = (
        (sums * (1.0 / math.sqrt(NLON)))
        .astype(jnp.bfloat16)
        .reshape(-1, var_dev, lat_dev, 2, m_window)
    )
    owned = lax.all_to_all(coefficients, "lat", split_axis=4, concat_axis=2, tiled=True)
    return jnp.einsum(
        "sin,lvirs->snrvl",
        legendre,
        lax.all_gather(owned, "lev", axis=0, tiled=True),
        preferred_element_type=jnp.float32,
    )


def axis_weights(x):
    square = x * x
    cubic = x * (square - 1.0) * (1.0 / 6.0)
    right = jnp.where(x > 0.0, cubic, 0.0)
    half = 0.5 * square
    half_x = 0.5 * x
    inner = half - 4.0 * right
    triple = 3.0 * cubic
    return [
        right - cubic,
        inner + (triple - half_x),
        (1.0 - square) + (6.0 * right - triple),
        inner + (half_x + cubic),
        right,
    ]


def column_kernel(
    main, prev, following, e_main, e_prev, e_following, top, bottom, departure, fractions,
    heating, coupling, basis, out, turned, edges, images, nearest, position, interp, state,
):
    levels, variables = main.shape[0], main.shape[1]
    rows = main.shape[2]
    pack = variables * BLOCKS
    block = pl.program_id(0)
    first = block == 0
    last = block == pl.num_programs(0) - 1
    lane = lax.broadcasted_iota(jnp.int32, (variables, BLOCKS, LANES), 2)
    sub = lax.broadcasted_iota(jnp.int32, (variables, BLOCKS, LANES), 1)

    def turn(values, start, v):
        count = values.shape[0]
        for jb in range(BLOCKS):
            turned[v, pl.ds(start * PITCH + jb, count, stride=PITCH), :] = values[
                :, jb * LANES : (jb + 1) * LANES
            ]

    def one_level(l, carry):
        for v in range(variables):
            width = BLOCKS * LANES
            turn(main[l, v].astype(jnp.float32), 8, v)
            before = prev[l, v].astype(jnp.float32)[8:16]
            turn(jnp.where(first, top[l, v, :, :width], before), 0, v)
            after = following[l, v].astype(jnp.float32)[0:8]
            turn(jnp.where(last, bottom[l, v, :, :width], after), 8 + rows, v)
            edges[v, 8 : 8 + rows] = e_main[l, v].astype(jnp.float32)
            before = e_prev[l, v].astype(jnp.float32)[8:16]
            edges[v, 0:8] = jnp.where(first, top[l, v, :, width:], before)
            after = e_following[l, v].astype(jnp.float32)[0:8]
            edges[v, 8 + rows : 16 + rows] = jnp.where(last, bottom[l, v, :, width:], after)
        code = departure[l]
        t_lat = fractions[0, l].astype(jnp.float32)
        t_lon = fractions[1, l].astype(jnp.float32)
        y = jnp.where(code >= 2, t_lat, t_lat - 1.0)
        x = jnp.where((code & 1) == 1, t_lon, t_lon - 1.0)
        for jb in range(BLOCKS):
            lanes = slice(jb * LANES, (jb + 1) * LANES)
            position[0, pl.ds(jb, rows, stride=PITCH), :] = y[:, lanes]
            position[1, pl.ds(jb, rows, stride=PITCH), :] = x[:, lanes]

        def make_images(w, carry):
            at = (w + 6) * PITCH
            values = jnp.stack([turned[v, pl.ds(at, BLOCKS), :] for v in range(variables)])
            edge = jnp.stack(
                [
                    jnp.broadcast_to(edges[v, pl.ds(w + 6, 1), :], (BLOCKS, LANES))
                    for v in range(variables)
                ]
            )
            ahead = jnp.where(sub == BLOCKS - 1, edge, pltpu.roll(values, BLOCKS - 1, 1))
            behind = jnp.where(sub == 0, edge, pltpu.roll(values, 1, 1))
            shifted = [
                pltpu.roll(jnp.where(lane >= LANES - 2, behind, values), 2, 2),
                pltpu.roll(jnp.where(lane >= LANES - 1, behind, values), 1, 2),
                values,
                pltpu.roll(jnp.where(lane < 1, ahead, values), LANES - 1, 2),
                pltpu.roll(jnp.where(lane < 2, ahead, values), LANES - 2, 2),
            ]
            for q in range(5):
                image = shifted[q].reshape(pack, LANES)
                images[q, w] = image.astype(jnp.bfloat16)
                if q in (1, 2, 3):
                    nearest[q - 1, w] = image
            return carry

        lax.fori_loop(0, rows + 4, make_images, 0, unroll=4)

        def interpolate(i, carry):
            at = i * PITCH
            row_w = axis_weights(position[0, pl.ds(at, BLOCKS), :])
            col_w = axis_weights(position[1, pl.ds(at, BLOCKS), :])
            row_w = [jnp.concatenate([w] * variables, axis=0) for w in row_w]
            col_w = [jnp.concatenate([w] * variables, axis=0) for w in col_w]
            row_n = [w.astype(jnp.bfloat16) for w in row_w]
            col_n = [w.astype(jnp.bfloat16) for w in col_w]
            outer = inner = None
            for r in range(5):
                line = col_n[0] * images[0, i + r] + col_n[4] * images[4, i + r]
                if r in (0, 4):
                    middle = [col_n[q] * images[q, i + r] for q in (1, 2, 3)]
                    line = (middle[0] + middle[1]) + (middle[2] + line)
                else:
                    near = [col_w[q] * nearest[q - 1, i + r] for q in (1, 2, 3)]
                    near = row_w[r] * (near[0] + near[1] + near[2])
                    inner = near if inner is None else inner + near
                line = row_n[r] * line
                outer = line if outer is None else outer + line
            total = inner + outer.astype(jnp.float32)
            for v in range(variables):
                interp[l, v, pl.ds(at, BLOCKS), :] = total[v * BLOCKS : (v + 1) * BLOCKS]
            return carry

        lax.fori_loop(0, rows, interpolate, 0, unroll=4)
        return carry

    lax.fori_loop(0, levels, one_level, 0)

    for v in range(variables):
        for jb in range(BLOCKS):
            lanes = slice(jb * LANES, (jb + 1) * LANES)
            field = jnp.concatenate(
                [interp[l, v, pl.ds(jb, rows, stride=PITCH), :] for l in range(levels)],
                axis=0,
            )
            column = jnp.dot(
                coupling[v], field.astype(jnp.bfloat16), preferred_element_type=jnp.float32
            )
            heat = jnp.concatenate([heating[v, :, lanes].astype(jnp.float32)] * levels, axis=0)
            state[:, lanes] = (field + heat * jnp.tanh(column)).astype(jnp.bfloat16)
        out[v, 0] = lax.dot_general(
            basis[...], state[...], (((1,), (1,)), ((), ())), preferred_element_type=jnp.float32
        )


def step_sums(upstream, departure, fractions, heating, mixing, basis):
    levels, variables, lat_dev, lon_dev = upstream.shape
    rows, near = ROWS, 16
    steps = lat_dev // rows
    peers = lax.axis_size("lev")
    up = [(i, (i + 1) % peers) for i in range(peers)]
    down = [(j, i) for i, j in up]
    left = lax.ppermute(upstream[..., lon_dev - 2 :], "lev", up)
    right = lax.ppermute(upstream[..., :2], "lev", down)
    gap = jnp.zeros((levels, variables, lat_dev, LANES - 4), upstream.dtype)
    edge = jnp.concatenate([right, gap, left], axis=3)
    bands = lax.axis_size("lat")
    north = [(i, i + 1) for i in range(bands - 1)]
    south = [(j, i) for i, j in north]
    lower = jnp.concatenate([upstream[:, :, lat_dev - 2 :], edge[:, :, lat_dev - 2 :]], axis=3)
    upper = jnp.concatenate([upstream[:, :, :2], edge[:, :, :2]], axis=3)
    top = lax.ppermute(lower, "lat", north).astype(jnp.float32)
    bottom = lax.ppermute(upper, "lat", south).astype(jnp.float32)
    top = jnp.pad(top, ((0, 0), (0, 0), (6, 0), (0, 0)))
    bottom = jnp.pad(bottom, ((0, 0), (0, 0), (0, 6), (0, 0)))
    unit = jnp.eye(rows, dtype=jnp.float32)
    coupling = (mixing[:, :, None, :, None] * unit[None, None, :, None, :]).reshape(
        variables, levels * rows, levels * rows
    )
    ratio = rows // near
    ends = lat_dev // near - 1

    def around(width):
        return [
            pl.BlockSpec((levels, variables, rows, width), lambda b: (0, 0, b, 0)),
            pl.BlockSpec(
                (levels, variables, near, width),
                lambda b: (0, 0, jnp.maximum(b * ratio - 1, 0), 0),
            ),
            pl.BlockSpec(
                (levels, variables, near, width),
                lambda b: (0, 0, jnp.minimum((b + 1) * ratio, ends), 0),
            ),
        ]

    def whole(shape):
        return pl.BlockSpec(shape, lambda b: (0,) * len(shape))

    pack = variables * BLOCKS
    slots = basis.shape[0]
    return pl.pallas_call(
        column_kernel,
        grid=(steps,),
        out_shape=jax.ShapeDtypeStruct((variables, steps, slots, levels * rows), jnp.float32),
        in_specs=around(lon_dev)
        + around(LANES)
        + [
            whole(top.shape),
            whole(bottom.shape),
            pl.BlockSpec((levels, rows, lon_dev), lambda b: (0, b, 0)),
            pl.BlockSpec((2, levels, rows, lon_dev), lambda b: (0, 0, b, 0)),
            pl.BlockSpec((variables, rows, lon_dev), lambda b: (0, b, 0)),
            whole(coupling.shape),
            whole(basis.shape),
        ],
        out_specs=pl.BlockSpec((variables, 1, slots, levels * rows), lambda b: (0, b, 0, 0)),
        scratch_shapes=[
            pltpu.VMEM((variables, (rows + 16) * PITCH + 8, LANES), jnp.float32),
            pltpu.VMEM((variables, rows + 16, LANES), jnp.float32),
            pltpu.VMEM((5, rows + 4, pack, LANES), jnp.bfloat16),
            pltpu.VMEM((3, rows + 4, pack, LANES), jnp.float32),
            pltpu.VMEM((2, rows * PITCH + 8, LANES), jnp.float32),
            pltpu.VMEM((levels, variables, rows * PITCH + 8, LANES), jnp.float32),
            pltpu.VMEM((levels * rows, lon_dev), jnp.bfloat16),
        ],
        compiler_params=pltpu.CompilerParams(vmem_limit_bytes=48 * 1024 * 1024),
    )(
        upstream, upstream, upstream, edge, edge, edge, top, bottom, departure, fractions,
        heating, coupling.astype(jnp.bfloat16), basis,
    )


def shards(upstream, departure, fractions, heating, mixing, slot_wavenumber, legendre):
    levels, var_dev, lat_dev, lon_dev = upstream.shape
    if lon_dev != BLOCKS * LANES or lat_dev % ROWS or var_dev * BLOCKS != 16:
        return shards_plain(
            upstream, departure, fractions, heating, mixing, slot_wavenumber, legendre
        )
    m_window = slot_wavenumber.shape[0]
    waves = slot_wavenumber * (NTRUNC // m_window)
    basis = fourier_basis(lax.axis_index("lev") * lon_dev, lon_dev, waves).T
    partial = step_sums(upstream, departure, fractions, heating, mixing, basis)
    sums = partial
    peers = lax.axis_size("lev")
    for hop in range(1, peers):
        sums = sums + lax.ppermute(partial, "lev", [(i, (i + hop) % peers) for i in range(peers)])
    steps = lat_dev // ROWS
    coefficients = (sums * (1.0 / math.sqrt(NLON))).astype(jnp.bfloat16)
    coefficients = coefficients.reshape(var_dev, steps, 2, m_window, levels * ROWS)
    owned = lax.all_to_all(coefficients, "lat", split_axis=3, concat_axis=1, tiled=True)
    slots, degrees = legendre.shape[0], legendre.shape[2]
    owned = owned.reshape(var_dev, -1, 2, slots, levels, ROWS)
    return jnp.einsum(
        "sbin,vbrsli->snrvl",
        legendre.reshape(slots, -1, ROWS, degrees),
        owned,
        preferred_element_type=jnp.float32,
    )


def solution(mesh):
    in_specs = (
        P("grp", "fld", "lat", "lev"),
        P("grp", "lat", "lev"),
        P(None, "grp", "lat", "lev"),
        P(("grp", "fld"), "lat", "lev"),
        P("fld", None, None),
        P(),
        P("lat", None, "lev"),
    )
    out_specs = P("lat", "lev", "grp", "fld", None)
    return jax.shard_map(shards, mesh=mesh, in_specs=in_specs, out_specs=out_specs, check_vma=False)
```
